32 devices in a mesh: dp: 4 (over y, x), ctx: 8 (over z, core).
Axes of the slice: x: 2, y: 2, z: 4, core: 2. Of those that a mesh axis runs over, the one named last changes fastest.
Arguments:
- phonemes: bfloat16 [4, 1024, 1024], P('dp', 'ctx'), may hold values from -6 to 6
- conv_kernel: float32 [7, 1024], replicated, may hold values from -2 to 2
- enc_gain: float32 [1024], replicated, may hold values from 0.1 to 1.9
- enc_in_weight: bfloat16 [1024, 1024], replicated, may hold values from -0.1875 to 0.1875
- enc_out_weight: bfloat16 [1024, 1024], replicated, may hold values from -0.1875 to 0.1875
- proj_weight: bfloat16 [1024, 1536], replicated, may hold values from -0.1875 to 0.1875
- hidden: bfloat16 [4, 4096, 1536], P('dp', 'ctx'), may hold values from -6 to 6
- durations: int32 [4, 1024], P('dp'), may hold values from 1 to 13, as said below
- utt_counts: int32 [4, 4], P('dp'), may hold values from 1 to 512, 1024 in all within a row
- timesteps: int32 [4, 4], P('dp'), may hold values from 0 to 999
- ada_weight: bfloat16 [256, 4608], replicated, may hold values from -0.375 to 0.375
- ff_in_weight: bfloat16 [1536, 2048], replicated, may hold values from -0.15625 to 0.15625
- ff_out_weight: bfloat16 [2048, 1536], replicated, may hold values from -0.125 to 0.125
- cotangent: bfloat16 [4, 4096, 1536], P('dp', 'ctx'), may hold values from -6 to 6
Outputs:
- transformer_layer_output: bfloat16 [4, 4096, 1536], P('dp', 'ctx')
- d_hidden: bfloat16 [4, 4096, 1536], P('dp', 'ctx')
- encoder_output_gradient: bfloat16 [4, 1024, 1024], P('dp', 'ctx')
- projection_weight_gradient: float32 [1024, 1536], P(('dp', 'ctx'))
The draws below stay inside these ranges and needn't reach their ends.
Inputs may be any that keep to these rules, and one draw needn't show every extreme that they name: In every replica the durations sum to 4096; the frames of the device at ctx index i are covered by phonemes i * 128 - 2 through (i + 1) * 128 + 1, and in every replica some device needs all 2 rows below its phonemes and some device all 2 rows above them; one duration is exactly 13. `utt_counts`: in every replica the counts sum to 1024 and one is exactly 512.
All inputs are finite; a program needn't handle non-finite values.
Results may differ from the reference program's by a relative error of at most 0.015.
Values may be sent and summed in bfloat16 or wider, within the bound.
A program may use at most 128 MiB of HBM per device.

```python
import math
import jax
import jax.numpy as jnp
import numpy as np
from jax import lax

DE = 1024
EF = 1024
DM = 1536
FFD = 2048
TE = 256
UTT = 4
PH_DEV = 128
PH_REP = 1024
FRAMES_REP = 4096
REPLICAS = 4
UTT_MOST = 512


def draw_durations(key, part):
    group_count = PH_REP // 4
    shard_count = PH_REP // PH_DEV

    def one_replica(replica_key):
        cut_key, wrap_key, place_key = jax.random.split(replica_key, 3)
        scores = jax.random.randint(cut_key, (group_count, 15), 0, 1 << 20) * 16 + jnp.arange(15, dtype=jnp.int32)[None, :]
        picked_values, picked = lax.top_k(scores, 3)
        cuts = jnp.sort(picked.astype(jnp.int32) + 1, axis=1)
        pieces = jnp.stack([cuts[:, 0], cuts[:, 1] - cuts[:, 0], cuts[:, 2] - cuts[:, 1], 16 - cuts[:, 2]], axis=1)
        wrap_parts = jax.random.randint(wrap_key, (2,), 1, 8)
        wrap_row = jnp.stack([wrap_parts[0], 8 - wrap_parts[0], wrap_parts[1], 8 - wrap_parts[1]])
        pieces = pieces.at[group_count - 1].set(wrap_row.astype(jnp.int32))
        order = jax.random.permutation(place_key, shard_count - 1).astype(jnp.int32) + 1
        patterns = jnp.array([[9, 1, 1, 5], [1, 1, 4, 10], [13, 1, 1, 1]], jnp.int32)
        for which in range(3):
            group_index = order[which] * PH_DEV // 4 - 1
            pieces = pieces.at[group_index].set(patterns[which])
        flat = pieces.reshape(-1)
        return jnp.roll(flat, 2).astype(jnp.int32)
    replica_keys = jax.random.split(key, REPLICAS)
    return jax.vmap(one_replica)(replica_keys).astype(jnp.int32)


def plant(values, stream_key, least, high):
    extent = values.shape
    place = [jax.random.randint(jax.random.fold_in(stream_key, axis), (), 0, extent[axis]) for axis in range(len(extent))]
    values = values.at[tuple(place)].set(least)
    longest = extent.index(max(extent))
    place[longest] = (place[longest] + 1) % extent[longest]
    return values.at[tuple(place)].set(high)


def block_scale(own_key, extent, shards, least, largest):
    def one(dim, blocks):
        heights = jax.random.uniform(jax.random.fold_in(jax.random.fold_in(own_key, 6), dim), (blocks,), jnp.float32, least / len(shards), largest / len(shards))
        return jnp.repeat(jnp.exp(heights), extent[dim] // blocks).reshape((-1,) + (1,) * (len(extent) - dim - 1))

    level = one(*shards[0])
    for cut in shards[1:]:
        level = level * one(*cut)
    return level


def split_up(count, total, reach, lean):
    weights = [(1 << 20) // math.isqrt(rank ** lean) + 1 for rank in range(2, count + 1)]
    surplus, holding = total - reach - (count - 1), [1] * (count - 1)
    while surplus > 0:
        candidates = [i for i in range(count - 1) if holding[i] < reach]
        pool, budget = sum([weights[i] for i in candidates]), surplus
        for i in candidates:
            extra = min(reach - holding[i], max(1, budget * weights[i] // pool), surplus)
            holding[i] = holding[i] + extra
            surplus = surplus - extra
    return np.array([reach] + holding)


def uneven(key, number_of, total, limit, skew):
    if number_of == 2:
        one = jax.random.randint(key, (), max(1, total - limit), min(limit, total - 1) + 1)
        return jnp.stack([one, total - one])
    sizes = jnp.asarray(split_up(number_of, total, limit, skew), jnp.int32)
    twos = (number_of - 1) // 2
    donor, sink = sizes[1:1 + 2 * twos:2], sizes[2:2 + 2 * twos:2]
    slack = jnp.minimum(donor - 1, limit - sink)
    moved = jax.random.randint(jax.random.fold_in(key, 1), (twos,), 0, 1 << 20) % (slack + 1)
    sizes = sizes.at[1:1 + 2 * twos:2].set(donor - moved).at[2:2 + 2 * twos:2].set(sink + moved)
    return sizes[jax.random.permutation(jax.random.fold_in(key, 2), number_of)]


def noise(own_key, dims, scale, most, cuts=(), held_as=jnp.bfloat16):
    result = scale * jax.random.normal(own_key, dims, jnp.float32)
    if cuts:
        result = result * block_scale(own_key, dims, cuts, -0.22, 0.18)
    return jnp.clip(result, -most, most).astype(held_as)


def setup_inputs(seed: int = 0) -> dict:
    key_of = jax.random.split(jax.random.key(seed), 15)
    return {
        "phonemes": noise(key_of[0], (REPLICAS, PH_REP, DE), 1.0, 6.0, ((0, 4), (1, 8))),
        "conv_kernel": noise(key_of[1], (7, DE), 0.4, 2.0, (), jnp.float32),
        "enc_gain": jnp.clip(1.0 + 0.18 * jax.random.normal(key_of[2], (DE,), jnp.float32), 0.1, 1.9),
        "enc_in_weight": noise(key_of[3], (DE, EF), DE ** -0.5, 0.1875),
        "enc_out_weight": noise(key_of[4], (EF, DE), EF ** -0.5, 0.1875),
        "proj_weight": noise(key_of[5], (DE, DM), DE ** -0.5, 0.1875),
        "hidden": noise(key_of[6], (REPLICAS, FRAMES_REP, DM), 1.0, 6.0, ((0, 4), (1, 8))),
        "durations": draw_durations(jax.random.fold_in(key_of[14], 71), 0),
        "utt_counts": jax.vmap(lambda own: uneven(own, UTT, PH_REP, UTT_MOST, 1))(jax.random.split(key_of[8], REPLICAS)).reshape((REPLICAS, UTT)).astype(jnp.int32),
        "timesteps": plant(jax.random.randint(key_of[9], (REPLICAS, UTT), 0, 1000), jax.random.fold_in(key_of[9], 1), 0, 999).astype(jnp.int32),
        "ada_weight": noise(key_of[10], (TE, 3 * DM), TE ** -0.5, 0.375),
        "ff_in_weight": noise(key_of[11], (DM, FFD), DM ** -0.5, 0.15625),
        "ff_out_weight": noise(key_of[12], (FFD, DM), FFD ** -0.5, 0.125),
        "cotangent": noise(key_of[13], (REPLICAS, FRAMES_REP, DM), 1.0, 6.0, ((0, 4), (1, 8))),
    }


tanh_scale = 0.7978845608028654

def gelu_value(inputs):
    inner = tanh_scale * (inputs + 0.044715 * inputs * inputs * inputs)
    return 0.5 * inputs * (1.0 + jnp.tanh(inner))

def gelu_slope(inputs):
    squared = inputs * inputs
    hyper = jnp.tanh(tanh_scale * (inputs + 0.044715 * squared * inputs))
    return 0.5 * (1.0 + hyper) + 0.5 * inputs * (1.0 - hyper * hyper) * tanh_scale * (1.0 + 3.0 * 0.044715 * squared)

def time_embed(timestep_ids, width):
    half_width = width // 2
    frequency = jnp.exp(-math.log(10000.0) * jnp.arange(half_width, dtype=jnp.float32) / half_width)
    angles = timestep_ids.astype(jnp.float32)[:, None] * frequency[None, :]
    return jnp.concatenate([jnp.sin(angles), jnp.cos(angles)], axis=1)

def rms_scale(values):
    return lax.rsqrt(lax.optimization_barrier(jnp.mean(values * values, axis=-1, keepdims=True)) + 1e-06)

def reference(phonemes, conv_kernel, enc_gain, enc_in_weight, enc_out_weight, proj_weight, hidden, durations, utt_counts, timesteps, ada_weight, ff_in_weight, ff_out_weight, cotangent):
    outputs = []
    hidden_grads = []
    encoded_grads = []
    proj_sum = jnp.zeros((DE, DM), jnp.float32)
    for replica in range(REPLICAS):
        phone_rows = phonemes[replica]
        utt_ends = jnp.cumsum(utt_counts[replica]).astype(jnp.int32)
        positions = jnp.arange(PH_REP, dtype=jnp.int32)
        segment = lax.optimization_barrier(jnp.sum((utt_ends[None, :] <= positions[:, None]).astype(jnp.int32), axis=1)).astype(jnp.int32)
        padded = jnp.pad(phone_rows.astype(jnp.float32), ((3, 3), (0, 0)))
        seg_padded = jnp.pad(segment, 3, constant_values=-1)
        mixed = jnp.zeros((PH_REP, DE), jnp.float32)
        for offset in range(7):
            same_utt = (seg_padded[offset:offset + PH_REP] == segment).astype(jnp.float32)
            mixed = mixed + conv_kernel[offset][None, :] * padded[offset:offset + PH_REP] * same_utt[:, None]
        normed = (mixed * rms_scale(mixed) * enc_gain[None, :]).astype(jnp.bfloat16)
        inner = gelu_value(jnp.dot(normed, enc_in_weight, preferred_element_type=jnp.float32)).astype(jnp.bfloat16)
        encoded = (phone_rows.astype(jnp.float32) + jnp.dot(inner, enc_out_weight, preferred_element_type=jnp.float32)).astype(jnp.bfloat16)
        cond = jnp.dot(encoded, proj_weight, preferred_element_type=jnp.float32).astype(jnp.bfloat16)
        phone_end = jnp.cumsum(durations[replica]).astype(jnp.int32)
        frames = jnp.arange(FRAMES_REP, dtype=jnp.int32)
        owner = jnp.searchsorted(phone_end, frames, side='right').astype(jnp.int32)
        cond_frames = cond[owner]
        utt_frame_end = phone_end[utt_ends - 1]
        utt_frame_begin = jnp.concatenate([jnp.zeros((1,), jnp.int32), utt_frame_end[:-1]])
        utt_onehot = ((frames[:, None] >= utt_frame_begin[None, :]) & (frames[:, None] < utt_frame_end[None, :])).astype(jnp.float32)
        act = jax.nn.silu(time_embed(timesteps[replica], TE)).astype(jnp.bfloat16)
        modul = jnp.dot(act, ada_weight, preferred_element_type=jnp.float32)
        frame_mod = jnp.dot(utt_onehot, modul, precision=lax.Precision.HIGHEST)
        shift = frame_mod[:, :DM]
        scale = frame_mod[:, DM:2 * DM]
        gate_values = frame_mod[:, 2 * DM:]
        residual_stream = hidden[replica].astype(jnp.float32) + cond_frames.astype(jnp.float32)
        rinv = rms_scale(residual_stream)
        normed2 = (residual_stream * rinv * (1.0 + scale) + shift).astype(jnp.bfloat16)
        pre = jnp.dot(normed2, ff_in_weight, preferred_element_type=jnp.float32)
        hidact = gelu_value(pre).astype(jnp.bfloat16)
        perceptron_output = jnp.dot(hidact, ff_out_weight, preferred_element_type=jnp.float32)
        outputs.append((residual_stream + gate_values * perceptron_output).astype(jnp.bfloat16))
        cot = cotangent[replica].astype(jnp.float32)
        d_mlp = (gate_values * cot).astype(jnp.bfloat16)
        d_act = jnp.dot(d_mlp, ff_out_weight.T, preferred_element_type=jnp.float32)
        d_pre = (d_act * gelu_slope(pre)).astype(jnp.bfloat16)
        d_norm = jnp.dot(d_pre, ff_in_weight.T, preferred_element_type=jnp.float32)
        d_hat = d_norm * (1.0 + scale)
        d_resid = cot + rinv * d_hat - residual_stream * rinv * rinv * rinv * lax.optimization_barrier(jnp.mean(d_hat * residual_stream, axis=-1, keepdims=True))
        frame_gradient_rows = d_resid.astype(jnp.bfloat16)
        hidden_grads.append(frame_gradient_rows)
        d_cond = jax.ops.segment_sum(frame_gradient_rows.astype(jnp.float32), owner, num_segments=PH_REP)
        encoded_grads.append(jnp.dot(d_cond, proj_weight.astype(jnp.float32).T, precision=lax.Precision.HIGHEST).astype(jnp.bfloat16))
        proj_sum = proj_sum + jnp.dot(encoded.astype(jnp.float32).T, d_cond, precision=lax.Precision.HIGHEST)
    projection_weight_gradient = proj_sum / math.sqrt(REPLICAS * FRAMES_REP)
    return (jnp.stack(outputs), jnp.stack(hidden_grads), jnp.stack(encoded_grads), projection_weight_gradient)
```

```python
import functools
import math

import jax
import jax.numpy as jnp
from jax import lax
from jax.experimental import pallas as pl
from jax.experimental.pallas import tpu as pltpu
from jax.sharding import PartitionSpec as P

HALO = 8
PIECES = 4
MESH = pl.DeviceIdType.MESH


tanh_scale = 0.7978845608028654


def extended_2(value, sides, width):
    for axis, dim in sides:
        size, length = (lax.axis_size(axis), value.shape[dim])
        up = [(i, (i + 1) % size) for i in range(size - 1)]
        down = [(j, i) for i, j in up]
        last = lax.slice_in_dim(value, length - width, length, axis=dim)
        initial = lax.slice_in_dim(value, 0, width, axis=dim)
        before = lax.ppermute(last, axis, up)
        after = lax.ppermute(initial, axis, down)
        value = jnp.concatenate([before, value, after], axis=dim)
    return value


def gelu_value(inputs):
    inner = tanh_scale * (inputs + 0.044715 * inputs * inputs * inputs)
    return 0.5 * inputs * (1.0 + jnp.tanh(inner))


def gelu_slope(inputs):
    squared = inputs * inputs
    hyper = jnp.tanh(tanh_scale * (inputs + 0.044715 * squared * inputs))
    return 0.5 * (1.0 + hyper) + 0.5 * inputs * (1.0 - hyper * hyper) * tanh_scale * (
        1.0 + 3.0 * 0.044715 * squared
    )


def time_embed(timestep_ids, width):
    half_width = width // 2
    frequency = jnp.exp(-math.log(10000.0) * jnp.arange(half_width, dtype=jnp.float32) / half_width)
    angles = timestep_ids.astype(jnp.float32)[:, None] * frequency[None, :]
    return jnp.concatenate([jnp.sin(angles), jnp.cos(angles)], axis=1)


def rms_scale(values):
    return lax.rsqrt(jnp.mean(values * values, axis=-1, keepdims=True) + 1e-06)


def contract_rows(left, right):
    return lax.dot_general(
        left, right, (((0,), (0,)), ((), ())), preferred_element_type=jnp.float32
    )


def contract_cols(left, right):
    return lax.dot_general(
        left, right, (((1,), (1,)), ((), ())), preferred_element_type=jnp.float32
    )


def reduce_kernel(
    dp_count,
    ctx_count,
    norm_factor,
    enc_ref,
    sums_ref,
    proj_ref,
    enc_grad_ref,
    proj_grad_ref,
    low_edge,
    high_edge,
    from_low,
    from_high,
    sums16,
    pair_enc,
    pair_sums,
    terms,
    first_in,
    second_out,
    second_in,
    chip_out,
    chip_in,
    edge_send,
    edge_recv,
    pair_send,
    pair_recv,
    first_send,
    first_recv,
    second_send,
    second_recv,
    chip_send,
    chip_recv,
):
    d = lax.axis_index("dp")
    c = lax.axis_index("ctx")
    core = lax.rem(c, 2)
    chip = c // 2
    chips = ctx_count // 2
    pair = c + 1 - 2 * core
    after = lax.rem(c + 1, ctx_count)
    before = lax.rem(c + ctx_count - 1, ctx_count)
    other = lax.rem(c + ctx_count - 1 + 2 * core, ctx_count)
    near = jnp.where(core == 0, d + 1 - 2 * lax.rem(d, 2), lax.rem(d + dp_count // 2, dp_count))
    far = jnp.where(core == 0, lax.rem(d + dp_count // 2, dp_count), d + 1 - 2 * lax.rem(d, 2))
    opposite = dp_count - 1 - d
    pieces, _, group_rows, cols = terms.shape
    rows = group_rows // chips
    phone_rows = enc_grad_ref.shape[0]
    window = sums_ref.shape[0]

    barrier = pltpu.get_barrier_semaphore()
    partners = [(d, pair), (d, other), (near, c), (far, c)]
    for i in range(1, chips):
        partners.append((d, lax.rem(c + 2 * i, ctx_count)))
    for partner in partners:
        pl.semaphore_signal(barrier, inc=1, device_id=partner, device_id_type=MESH)

    sums16[...] = sums_ref[...].astype(jnp.bfloat16)
    low_edge[...] = sums_ref[:HALO, :]
    high_edge[...] = sums_ref[window - HALO :, :]
    pl.semaphore_wait(barrier, len(partners))

    def remote(src, dst, send, recv, target):
        return pltpu.make_async_remote_copy(
            src_ref=src,
            dst_ref=dst,
            send_sem=send,
            recv_sem=recv,
            device_id=target,
            device_id_type=MESH,
        )

    pair_copies = [
        remote(sums16, pair_sums, pair_send.at[0], pair_recv.at[0], (d, pair)),
        remote(enc_ref.at[1 - core], pair_enc, pair_send.at[1], pair_recv.at[1], (d, pair)),
    ]
    edge_copies = [
        remote(low_edge, from_high, edge_send.at[0], edge_recv.at[0], (d, before)),
        remote(high_edge, from_low, edge_send.at[1], edge_recv.at[1], (d, after)),
    ]
    for copy in pair_copies + edge_copies:
        copy.start()
    for copy in pair_copies:
        copy.wait_recv()

    own_enc = enc_ref[core]
    their_enc = pair_enc[...]
    first = []
    for q in range(pieces):
        at = slice(q * cols, (q + 1) * cols)
        term = jnp.dot(own_enc, sums16[:, at], preferred_element_type=jnp.float32)
        term = term + jnp.dot(their_enc, pair_sums[:, at], preferred_element_type=jnp.float32)
        terms[q] = term.astype(jnp.bfloat16).reshape(dp_count, group_rows, cols)
        for i, group in ((1, opposite), (0, near)):
            copy = remote(
                terms.at[q, group],
                first_in.at[q, i],
                first_send.at[q, i],
                first_recv.at[q, i],
                (near, c),
            )
            copy.start()
            first.append((q, i, copy))
    arrived = {(q, i): copy for q, i, copy in first}

    for copy in edge_copies:
        copy.wait_recv()
    own = sums_ref[HALO : HALO + phone_rows, :]
    d_cond = jnp.concatenate(
        [
            own[:HALO] + from_low[...],
            own[HALO : phone_rows - HALO],
            own[phone_rows - HALO :] + from_high[...],
        ],
        axis=0,
    ).astype(jnp.bfloat16)
    enc_grad_ref[...] = contract_cols(d_cond, proj_ref[...]).astype(jnp.bfloat16)

    second = []
    chip_copies = []
    for q in range(pieces + 1):
        if q < pieces:
            arrived[q, 1].wait_recv()
            second_out[q] = (
                terms[q, far].astype(jnp.float32) + first_in[q, 1].astype(jnp.float32)
            ).astype(jnp.bfloat16)
            copy = remote(
                second_out.at[q], second_in.at[q], second_send.at[q], second_recv.at[q], (far, c)
            )
            copy.start()
            second.append(copy)
        if q >= 1:
            p = q - 1
            arrived[p, 0].wait_recv()
            second[p].wait_recv()
            total = (
                terms[p, d].astype(jnp.float32)
                + first_in[p, 0].astype(jnp.float32)
                + second_in[p].astype(jnp.float32)
            )
            chip_out[p] = total.reshape(chips, rows, cols).astype(jnp.bfloat16)
            for i in range(1, chips):
                target = lax.rem(chip + i, chips)
                copy = remote(
                    chip_out.at[p, target],
                    chip_in.at[p, i],
                    chip_send.at[p, i],
                    chip_recv.at[p, i],
                    (d, 2 * target + core),
                )
                copy.start()
                chip_copies.append((p, copy))
    for q in range(pieces):
        total = chip_out[q, chip].astype(jnp.float32)
        i = 1
        for p, copy in chip_copies:
            if p == q:
                copy.wait_recv()
                total = total + chip_in[q, i].astype(jnp.float32)
                i += 1
        proj_grad_ref[:, q * cols : (q + 1) * cols] = total * norm_factor
    for copy in pair_copies + edge_copies + second:
        copy.wait_send()
    for _, _, copy in first:
        copy.wait_send()
    for _, copy in chip_copies:
        copy.wait_send()


def reduce_gradients(enc_window, window_sums, proj_weight, phone_local, norm_factor):
    dp_count, ctx_count = lax.axis_size("dp"), lax.axis_size("ctx")
    chips = ctx_count // 2
    window, enc_width = enc_window.shape
    width = window_sums.shape[1]
    rows = enc_width // (dp_count * ctx_count)
    group_rows = chips * rows
    cols = width // PIECES
    enc_halves = (
        enc_window.T.reshape(dp_count * chips, 2, rows, window)
        .transpose(1, 0, 2, 3)
        .reshape(2, enc_width // 2, window)
    )
    vmem = pl.BlockSpec(memory_space=pltpu.VMEM)
    bf16, f32, dma = jnp.bfloat16, jnp.float32, pltpu.SemaphoreType.DMA
    return pl.pallas_call(
        functools.partial(reduce_kernel, dp_count, ctx_count, norm_factor),
        out_shape=(
            jax.ShapeDtypeStruct((phone_local, enc_width), bf16),
            jax.ShapeDtypeStruct((rows, width), f32),
        ),
        in_specs=[vmem] * 3,
        out_specs=(vmem, vmem),
        scratch_shapes=[
            pltpu.VMEM((HALO, width), f32),
            pltpu.VMEM((HALO, width), f32),
            pltpu.VMEM((HALO, width), f32),
            pltpu.VMEM((HALO, width), f32),
            pltpu.VMEM((window, width), bf16),
            pltpu.VMEM((enc_width // 2, window), bf16),
            pltpu.VMEM((window, width), bf16),
            pltpu.VMEM((PIECES, dp_count, group_rows, cols), bf16),
            pltpu.VMEM((PIECES, 2, group_rows, cols), bf16),
            pltpu.VMEM((PIECES, group_rows, cols), bf16),
            pltpu.VMEM((PIECES, group_rows, cols), bf16),
            pltpu.VMEM((PIECES, chips, rows, cols), bf16),
            pltpu.VMEM((PIECES, chips, rows, cols), bf16),
            dma((2,)),
            dma((2,)),
            dma((2,)),
            dma((2,)),
            dma((PIECES, 2)),
            dma((PIECES, 2)),
            dma((PIECES,)),
            dma((PIECES,)),
            dma((PIECES, chips)),
            dma((PIECES, chips)),
        ],
        compiler_params=pltpu.CompilerParams(
            collective_id=0, has_side_effects=True, vmem_limit_bytes=40 * 1024 * 1024
        ),
        name="reduce_gradients",
    )(enc_halves, window_sums, proj_weight)


def shards(
    phonemes,
    conv_kernel,
    enc_gain,
    enc_in_weight,
    enc_out_weight,
    proj_weight,
    hidden,
    durations,
    utt_counts,
    timesteps,
    ada_weight,
    ff_in_weight,
    ff_out_weight,
    cotangent,
):
    ctx_index = lax.axis_index("ctx")
    ctx_count = lax.axis_size("ctx")
    dp_count = lax.axis_size("dp")
    phone_rows = phonemes[0]
    phone_local = phone_rows.shape[0]
    frame_local = hidden.shape[1]
    model_width = hidden.shape[2]
    utt_ends = jnp.cumsum(utt_counts[0])
    window_rows = phone_local + 2 * HALO
    extended = extended_2(phone_rows, (("ctx", 0),), HALO + 3)
    positions = ctx_index * phone_local - HALO - 3 + jnp.arange(window_rows + 6, dtype=jnp.int32)
    segment = jnp.sum((utt_ends[None, :] <= positions[:, None]).astype(jnp.int32), axis=1)
    centre = segment[3 : 3 + window_rows]
    mixed = jnp.zeros((window_rows, phone_rows.shape[1]), jnp.float32)
    for offset in range(7):
        same_utt = (segment[offset : offset + window_rows] == centre).astype(jnp.float32)
        mixed = (
            mixed
            + conv_kernel[offset][None, :]
            * extended[offset : offset + window_rows].astype(jnp.float32)
            * same_utt[:, None]
        )
    normed = (mixed * rms_scale(mixed) * enc_gain[None, :]).astype(jnp.bfloat16)
    inner = gelu_value(jnp.dot(normed, enc_in_weight, preferred_element_type=jnp.float32)).astype(
        jnp.bfloat16
    )
    encoded = (
        extended[3 : 3 + window_rows].astype(jnp.float32)
        + jnp.dot(inner, enc_out_weight, preferred_element_type=jnp.float32)
    ).astype(jnp.bfloat16)
    phone_dur = durations[0]
    phone_end = jnp.cumsum(phone_dur)
    phone_begin = phone_end - phone_dur
    frame_ids = ctx_index * frame_local + jnp.arange(frame_local, dtype=jnp.int32)
    begin_padded = jnp.pad(phone_begin, HALO, constant_values=-1)
    end_padded = jnp.pad(phone_end, HALO, constant_values=-1)
    begin_window = lax.dynamic_slice_in_dim(begin_padded, ctx_index * phone_local, window_rows)
    end_window = lax.dynamic_slice_in_dim(end_padded, ctx_index * phone_local, window_rows)
    onehot = (
        (frame_ids[:, None] >= begin_window[None, :]) & (frame_ids[:, None] < end_window[None, :])
    ).astype(jnp.bfloat16)
    cond_window = jnp.dot(encoded, proj_weight, preferred_element_type=jnp.float32).astype(
        jnp.bfloat16
    )
    cond_frames = jnp.dot(onehot, cond_window, preferred_element_type=jnp.float32).astype(
        jnp.bfloat16
    )
    utt_marks = (
        jnp.arange(phone_dur.shape[0], dtype=jnp.int32)[None, :] < utt_ends[:, None]
    ).astype(jnp.int32)
    utt_frame_end = jnp.sum(utt_marks * phone_dur[None, :], axis=1)
    utt_frame_begin = jnp.concatenate([jnp.zeros((1,), jnp.int32), utt_frame_end[:-1]])
    utt_onehot = (
        (frame_ids[:, None] >= utt_frame_begin[None, :])
        & (frame_ids[:, None] < utt_frame_end[None, :])
    ).astype(jnp.float32)
    act = jax.nn.silu(time_embed(timesteps[0], ada_weight.shape[0])).astype(jnp.bfloat16)
    modul = jnp.dot(act, ada_weight, preferred_element_type=jnp.float32)
    frame_mod = jnp.dot(utt_onehot, modul, precision=lax.Precision.HIGHEST)
    shift = frame_mod[:, :model_width]
    scale = frame_mod[:, model_width : 2 * model_width]
    gate_values = frame_mod[:, 2 * model_width :]
    residual_stream = hidden[0].astype(jnp.float32) + cond_frames.astype(jnp.float32)
    rinv = rms_scale(residual_stream)
    normed2 = (residual_stream * rinv * (1.0 + scale) + shift).astype(jnp.bfloat16)
    pre = jnp.dot(normed2, ff_in_weight, preferred_element_type=jnp.float32)
    hidact = gelu_value(pre).astype(jnp.bfloat16)
    perceptron_output = jnp.dot(hidact, ff_out_weight, preferred_element_type=jnp.float32)
    transformer_layer_output = (residual_stream + gate_values * perceptron_output).astype(
        jnp.bfloat16
    )
    cot = cotangent[0].astype(jnp.float32)
    d_mlp = (gate_values * cot).astype(jnp.bfloat16)
    d_act = contract_cols(d_mlp, ff_out_weight)
    d_pre = (d_act * gelu_slope(pre)).astype(jnp.bfloat16)
    d_norm = contract_cols(d_pre, ff_in_weight)
    d_hat = d_norm * (1.0 + scale)
    d_resid = (
        cot
        + rinv * d_hat
        - residual_stream
        * rinv
        * rinv
        * rinv
        * jnp.mean(d_hat * residual_stream, axis=-1, keepdims=True)
    )
    frame_gradient_rows = d_resid.astype(jnp.bfloat16)
    window_sums = contract_rows(onehot, frame_gradient_rows)
    norm_factor = 1.0 / math.sqrt(dp_count * ctx_count * frame_local)
    encoder_output_gradient, projection_weight_gradient = reduce_gradients(
        encoded, window_sums, proj_weight, phone_local, norm_factor
    )
    return (
        transformer_layer_output[None],
        frame_gradient_rows[None],
        encoder_output_gradient[None],
        projection_weight_gradient,
    )


def solution(mesh):
    in_specs = (
        P("dp", "ctx", None),
        P(),
        P(),
        P(),
        P(),
        P(),
        P("dp", "ctx", None),
        P("dp", None),
        P("dp", None),
        P("dp", None),
        P(),
        P(),
        P(),
        P("dp", "ctx", None),
    )
    out_specs = (
        P("dp", "ctx", None),
        P("dp", "ctx", None),
        P("dp", "ctx", None),
        P(("dp", "ctx"), None),
    )
    return jax.shard_map(shards, mesh=mesh, in_specs=in_specs, out_specs=out_specs, check_vma=False)
```

```python
import functools
import math

import jax
import jax.numpy as jnp
from jax import lax
from jax.experimental import pallas as pl
from jax.experimental.pallas import tpu as pltpu
from jax.sharding import PartitionSpec as P

HALO = 8
PIECES = 4
NARROW = 256
WIDE = 512
MESH = pl.DeviceIdType.MESH


tanh_scale = 0.7978845608028654


def extended_2(value, sides, width):
    for axis, dim in sides:
        size, length = (lax.axis_size(axis), value.shape[dim])
        up = [(i, (i + 1) % size) for i in range(size - 1)]
        down = [(j, i) for i, j in up]
        last = lax.slice_in_dim(value, length - width, length, axis=dim)
        initial = lax.slice_in_dim(value, 0, width, axis=dim)
        before = lax.ppermute(last, axis, up)
        after = lax.ppermute(initial, axis, down)
        value = jnp.concatenate([before, value, after], axis=dim)
    return value


def gelu_value(inputs):
    inner = tanh_scale * (inputs + 0.044715 * inputs * inputs * inputs)
    return 0.5 * inputs * (1.0 + jnp.tanh(inner))


def time_embed(timestep_ids, width):
    half_width = width // 2
    frequency = jnp.exp(-math.log(10000.0) * jnp.arange(half_width, dtype=jnp.float32) / half_width)
    angles = timestep_ids.astype(jnp.float32)[:, None] * frequency[None, :]
    return jnp.concatenate([jnp.sin(angles), jnp.cos(angles)], axis=1)


def rms_scale(values):
    return lax.rsqrt(jnp.mean(values * values, axis=-1, keepdims=True) + 1e-06)


def contract_cols(left, right):
    return lax.dot_general(
        left, right, (((1,), (1,)), ((), ())), preferred_element_type=jnp.float32
    )


def reduce_kernel(
    dp_count,
    ctx_count,
    norm_factor,
    enc_ref,
    sums_ref,
    proj_ref,
    enc_grad_ref,
    proj_grad_ref,
    low_edge,
    high_edge,
    from_low,
    from_high,
    sums16,
    pair_enc,
    pair_sums,
    terms,
    first_in,
    second_out,
    second_in,
    chip_out,
    chip_in,
    edge_send,
    edge_recv,
    pair_send,
    pair_recv,
    first_send,
    first_recv,
    second_send,
    second_recv,
    chip_send,
    chip_recv,
):
    d = lax.axis_index("dp")
    c = lax.axis_index("ctx")
    core = lax.rem(c, 2)
    chip = c // 2
    chips = ctx_count // 2
    pair = c + 1 - 2 * core
    after = lax.rem(c + 1, ctx_count)
    before = lax.rem(c + ctx_count - 1, ctx_count)
    other = lax.rem(c + ctx_count - 1 + 2 * core, ctx_count)
    near = jnp.where(core == 0, d + 1 - 2 * lax.rem(d, 2), lax.rem(d + dp_count // 2, dp_count))
    far = jnp.where(core == 0, lax.rem(d + dp_count // 2, dp_count), d + 1 - 2 * lax.rem(d, 2))
    opposite = dp_count - 1 - d
    pieces, _, group_rows, cols = terms.shape
    rows = group_rows // chips
    phone_rows = enc_grad_ref.shape[0]
    window = sums_ref.shape[0]

    barrier = pltpu.get_barrier_semaphore()
    partners = [(d, pair), (d, other), (near, c), (far, c)]
    for i in range(1, chips):
        partners.append((d, lax.rem(c + 2 * i, ctx_count)))
    for partner in partners:
        pl.semaphore_signal(barrier, inc=1, device_id=partner, device_id_type=MESH)

    sums16[...] = sums_ref[...].astype(jnp.bfloat16)
    low_edge[...] = sums_ref[:HALO, :]
    high_edge[...] = sums_ref[window - HALO :, :]
    pl.semaphore_wait(barrier, len(partners))

    def remote(src, dst, send, recv, target):
        return pltpu.make_async_remote_copy(
            src_ref=src,
            dst_ref=dst,
            send_sem=send,
            recv_sem=recv,
            device_id=target,
            device_id_type=MESH,
        )

    pair_copies = [
        remote(sums16, pair_sums, pair_send.at[0], pair_recv.at[0], (d, pair)),
        remote(enc_ref.at[1 - core], pair_enc, pair_send.at[1], pair_recv.at[1], (d, pair)),
    ]
    edge_copies = [
        remote(low_edge, from_high, edge_send.at[0], edge_recv.at[0], (d, before)),
        remote(high_edge, from_low, edge_send.at[1], edge_recv.at[1], (d, after)),
    ]
    for copy in pair_copies + edge_copies:
        copy.start()
    for copy in pair_copies:
        copy.wait_recv()

    own_enc = enc_ref[core]
    their_enc = pair_enc[...]
    first = []
    for q in range(pieces):
        at = slice(q * cols, (q + 1) * cols)
        term = jnp.dot(own_enc, sums16[:, at], preferred_element_type=jnp.float32)
        term = term + jnp.dot(their_enc, pair_sums[:, at], preferred_element_type=jnp.float32)
        terms[q] = term.astype(jnp.bfloat16).reshape(dp_count, group_rows, cols)
        for i, group in ((1, opposite), (0, near)):
            copy = remote(
                terms.at[q, group],
                first_in.at[q, i],
                first_send.at[q, i],
                first_recv.at[q, i],
                (near, c),
            )
            copy.start()
            first.append((q, i, copy))
    arrived = {(q, i): copy for q, i, copy in first}

    for copy in edge_copies:
        copy.wait_recv()
    own = sums_ref[HALO : HALO + phone_rows, :]
    d_cond = jnp.concatenate(
        [
            own[:HALO] + from_low[...],
            own[HALO : phone_rows - HALO],
            own[phone_rows - HALO :] + from_high[...],
        ],
        axis=0,
    ).astype(jnp.bfloat16)
    enc_grad_ref[...] = contract_cols(d_cond, proj_ref[...]).astype(jnp.bfloat16)

    second = []
    chip_copies = []
    for q in range(pieces + 1):
        if q < pieces:
            arrived[q, 1].wait_recv()
            second_out[q] = (
                terms[q, far].astype(jnp.float32) + first_in[q, 1].astype(jnp.float32)
            ).astype(jnp.bfloat16)
            copy = remote(
                second_out.at[q], second_in.at[q], second_send.at[q], second_recv.at[q], (far, c)
            )
            copy.start()
            second.append(copy)
        if q >= 1:
            p = q - 1
            arrived[p, 0].wait_recv()
            second[p].wait_recv()
            total = (
                terms[p, d].astype(jnp.float32)
                + first_in[p, 0].astype(jnp.float32)
                + second_in[p].astype(jnp.float32)
            )
            chip_out[p] = total.reshape(chips, rows, cols).astype(jnp.bfloat16)
            for i in range(1, chips):
                target = lax.rem(chip + i, chips)
                copy = remote(
                    chip_out.at[p, target],
                    chip_in.at[p, i],
                    chip_send.at[p, i],
                    chip_recv.at[p, i],
                    (d, 2 * target + core),
                )
                copy.start()
                chip_copies.append((p, copy))
    for q in range(pieces):
        total = chip_out[q, chip].astype(jnp.float32)
        i = 1
        for p, copy in chip_copies:
            if p == q:
                copy.wait_recv()
                total = total + chip_in[q, i].astype(jnp.float32)
                i += 1
        proj_grad_ref[:, q * cols : (q + 1) * cols] = total * norm_factor
    for copy in pair_copies + edge_copies + second:
        copy.wait_send()
    for _, _, copy in first:
        copy.wait_send()
    for _, copy in chip_copies:
        copy.wait_send()


def reduce_gradients(enc_halves, window_sums, proj_weight, phone_local, norm_factor):
    dp_count, ctx_count = lax.axis_size("dp"), lax.axis_size("ctx")
    chips = ctx_count // 2
    enc_width = proj_weight.shape[0]
    window, width = window_sums.shape
    rows = enc_width // (dp_count * ctx_count)
    group_rows = chips * rows
    cols = width // PIECES
    vmem = pl.BlockSpec(memory_space=pltpu.VMEM)
    bf16, f32, dma = jnp.bfloat16, jnp.float32, pltpu.SemaphoreType.DMA
    return pl.pallas_call(
        functools.partial(reduce_kernel, dp_count, ctx_count, norm_factor),
        out_shape=(
            jax.ShapeDtypeStruct((phone_local, enc_width), bf16),
            jax.ShapeDtypeStruct((rows, width), f32),
        ),
        in_specs=[vmem] * 3,
        out_specs=(vmem, vmem),
        scratch_shapes=[
            pltpu.VMEM((HALO, width), f32),
            pltpu.VMEM((HALO, width), f32),
            pltpu.VMEM((HALO, width), f32),
            pltpu.VMEM((HALO, width), f32),
            pltpu.VMEM((window, width), bf16),
            pltpu.VMEM((enc_width // 2, window), bf16),
            pltpu.VMEM((window, width), bf16),
            pltpu.VMEM((PIECES, dp_count, group_rows, cols), bf16),
            pltpu.VMEM((PIECES, 2, group_rows, cols), bf16),
            pltpu.VMEM((PIECES, group_rows, cols), bf16),
            pltpu.VMEM((PIECES, group_rows, cols), bf16),
            pltpu.VMEM((PIECES, chips, rows, cols), bf16),
            pltpu.VMEM((PIECES, chips, rows, cols), bf16),
            dma((2,)),
            dma((2,)),
            dma((2,)),
            dma((2,)),
            dma((PIECES, 2)),
            dma((PIECES, 2)),
            dma((PIECES,)),
            dma((PIECES,)),
            dma((PIECES, chips)),
            dma((PIECES, chips)),
        ],
        compiler_params=pltpu.CompilerParams(
            collective_id=0, has_side_effects=True, vmem_limit_bytes=40 * 1024 * 1024
        ),
        name="reduce_gradients",
    )(enc_halves.reshape(2, enc_width // 2, window), window_sums, proj_weight)


def gelu_parts(inputs):
    squared = inputs * inputs
    hyper = jnp.tanh(tanh_scale * (inputs + 0.044715 * squared * inputs))
    half = 0.5 * (1.0 + hyper)
    slope = half + 0.5 * inputs * (1.0 - hyper * hyper) * tanh_scale * (
        1.0 + 3.0 * 0.044715 * squared
    )
    return inputs * half, slope


def layer_kernel(
    ends_ref,
    ext_ref,
    mask_ref,
    spans_row_ref,
    spans_col_ref,
    act_ref,
    conv_ref,
    gain_ref,
    enc_in_hbm,
    enc_out_hbm,
    proj_hbm,
    ada_hbm,
    ff_in_hbm,
    ff_out_hbm,
    hidden_hbm,
    cot_hbm,
    out_hbm,
    d_hidden_hbm,
    sums_ref,
    halves_ref,
    enc_in,
    enc_out,
    proj,
    ada,
    ff_in,
    ff_out,
    hidden,
    cot,
    ext32,
    modul,
    resid,
    normed2,
    d_mlp,
    hidact,
    d_pre,
    d_hat,
    out_buf,
    d_hidden,
    sems,
):
    pairs = (
        (enc_in_hbm, enc_in),
        (enc_out_hbm, enc_out),
        (proj_hbm, proj),
        (ada_hbm, ada),
        (hidden_hbm.at[0], hidden),
        (cot_hbm.at[0], cot),
        (ff_in_hbm, ff_in),
        (ff_out_hbm, ff_out),
    )
    loads = [pltpu.make_async_copy(a, b, sems.at[i]) for i, (a, b) in enumerate(pairs)]
    for load in loads:
        load.start()
    utts = ends_ref.shape[0]
    frames, width = resid.shape
    inner_width = hidact.shape[1]
    window = mask_ref.shape[0]
    groups = halves_ref.shape[1]

    ext32[...] = ext_ref[...].astype(jnp.float32)
    mixed = jnp.zeros((window, ext32.shape[1]), jnp.float32)
    for k in range(7):
        mixed = mixed + conv_ref[k : k + 1, :] * ext32[k : k + window, :] * mask_ref[:, k : k + 1]
    normed = (mixed * rms_scale(mixed) * gain_ref[...]).astype(jnp.bfloat16)
    loads[0].wait()
    inner = gelu_value(
        jnp.dot(normed, enc_in[...], preferred_element_type=jnp.float32)
    ).astype(jnp.bfloat16)
    loads[1].wait()
    encoded = (
        ext32[3 : 3 + window, :]
        + jnp.dot(inner, enc_out[...], preferred_element_type=jnp.float32)
    ).astype(jnp.bfloat16)
    turned = encoded.astype(jnp.float32).T.reshape(groups, 2, -1, window)
    for half in range(2):
        halves_ref[half] = turned[:, half].astype(jnp.bfloat16)
    loads[2].wait()
    cond = jnp.dot(encoded, proj[...], preferred_element_type=jnp.float32).astype(jnp.bfloat16)
    loads[3].wait()
    modul[...] = jnp.dot(act_ref[...], ada[...], preferred_element_type=jnp.float32)

    def pick(which, at, step):
        rows = modul[:, which * width + at : which * width + at + step]
        frame = lax.broadcasted_iota(jnp.int32, (frames, step), 0)
        value = jnp.broadcast_to(rows[utts - 1 : utts], (frames, step))
        for u in reversed(range(utts - 1)):
            value = jnp.where(frame < ends_ref[u], rows[u : u + 1], value)
        return value

    frame_rows = lax.broadcasted_iota(jnp.int32, (frames, window), 0)
    onehot = jnp.where(
        (frame_rows >= spans_row_ref[0:1, :]) & (frame_rows < spans_row_ref[1:2, :]), 1.0, 0.0
    ).astype(jnp.bfloat16)
    step = NARROW
    loads[4].wait()
    square = jnp.zeros((frames, 1), jnp.float32)
    for at in range(0, width, step):
        cond_frames = jnp.dot(
            onehot, cond[:, at : at + step], preferred_element_type=jnp.float32
        )
        value = hidden[:, at : at + step].astype(jnp.float32) + cond_frames
        resid[:, at : at + step] = value
        square = square + jnp.sum(value * value, axis=-1, keepdims=True)
    rinv = lax.rsqrt(square * (1.0 / width) + 1e-06)
    loads[5].wait()
    for at in range(0, width, step):
        cols = slice(at, at + step)
        normed2[:, cols] = (
            resid[:, cols] * rinv * (1.0 + pick(1, at, step)) + pick(0, at, step)
        ).astype(jnp.bfloat16)
        d_mlp[:, cols] = (pick(2, at, step) * cot[:, cols].astype(jnp.float32)).astype(
            jnp.bfloat16
        )
    loads[6].wait()
    loads[7].wait()
    for at in range(0, inner_width, WIDE):
        cols = slice(at, at + WIDE)
        pre = jnp.dot(normed2[...], ff_in[:, cols], preferred_element_type=jnp.float32)
        value, slope = gelu_parts(pre)
        hidact[:, cols] = value.astype(jnp.bfloat16)
        d_act = contract_cols(d_mlp[...], ff_out[cols, :])
        d_pre[:, cols] = (d_act * slope).astype(jnp.bfloat16)
    for at in range(0, width, step):
        cols = slice(at, at + step)
        mlp = jnp.dot(hidact[...], ff_out[:, cols], preferred_element_type=jnp.float32)
        out_buf[:, cols] = (resid[:, cols] + pick(2, at, step) * mlp).astype(jnp.bfloat16)
    out_store = pltpu.make_async_copy(out_buf, out_hbm.at[0], sems.at[8])
    out_store.start()
    inside = jnp.zeros((frames, 1), jnp.float32)
    for at in range(0, width, step):
        cols = slice(at, at + step)
        value = contract_cols(d_pre[...], ff_in[cols, :]) * (1.0 + pick(1, at, step))
        d_hat[:, cols] = value
        inside = inside + jnp.sum(value * resid[:, cols], axis=-1, keepdims=True)
    factor = rinv * rinv * rinv * (inside * (1.0 / width))
    for at in range(0, width, step):
        cols = slice(at, at + step)
        d_hidden[:, cols] = (
            cot[:, cols].astype(jnp.float32) + rinv * d_hat[:, cols] - resid[:, cols] * factor
        ).astype(jnp.bfloat16)
    d_store = pltpu.make_async_copy(d_hidden, d_hidden_hbm.at[0], sems.at[9])
    d_store.start()
    frame_cols = lax.broadcasted_iota(jnp.int32, (window, frames), 1)
    turned_onehot = jnp.where(
        (frame_cols >= spans_col_ref[:, 0:1]) & (frame_cols < spans_col_ref[:, 1:2]), 1.0, 0.0
    ).astype(jnp.bfloat16)
    for at in range(0, width, step):
        cols = slice(at, at + step)
        sums_ref[:, cols] = jnp.dot(
            turned_onehot, d_hidden[:, cols], preferred_element_type=jnp.float32
        )
    out_store.wait()
    d_store.wait()


def layers(
    ends,
    extended,
    masks,
    spans,
    act,
    conv_kernel,
    enc_gain,
    enc_in_weight,
    enc_out_weight,
    proj_weight,
    ada_weight,
    ff_in_weight,
    ff_out_weight,
    hidden,
    cotangent,
    groups,
):
    frames, width = hidden.shape[1:]
    enc_width, inner_width = conv_kernel.shape[1], ff_in_weight.shape[1]
    window = masks.shape[0]
    vmem = pl.BlockSpec(memory_space=pltpu.VMEM)
    hbm = pl.BlockSpec(memory_space=pl.ANY)
    bf16, f32 = jnp.bfloat16, jnp.float32
    flat = (enc_in_weight, enc_out_weight, proj_weight, ada_weight, ff_in_weight, ff_out_weight)
    return pl.pallas_call(
        layer_kernel,
        out_shape=(
            jax.ShapeDtypeStruct((1, frames, width), bf16),
            jax.ShapeDtypeStruct((1, frames, width), bf16),
            jax.ShapeDtypeStruct((window, width), f32),
            jax.ShapeDtypeStruct((2, groups, enc_width // (2 * groups), window), bf16),
        ),
        in_specs=[pl.BlockSpec(memory_space=pltpu.SMEM)] + [vmem] * 7 + [hbm] * 8,
        out_specs=(hbm, hbm, vmem, vmem),
        scratch_shapes=[pltpu.VMEM(a.shape, bf16) for a in flat]
        + [
            pltpu.VMEM((frames, width), bf16),
            pltpu.VMEM((frames, width), bf16),
            pltpu.VMEM(extended.shape, f32),
            pltpu.VMEM((act.shape[0], ada_weight.shape[1]), f32),
            pltpu.VMEM((frames, width), f32),
            pltpu.VMEM((frames, width), bf16),
            pltpu.VMEM((frames, width), bf16),
            pltpu.VMEM((frames, inner_width), bf16),
            pltpu.VMEM((frames, inner_width), bf16),
            pltpu.VMEM((frames, width), f32),
            pltpu.VMEM((frames, width), bf16),
            pltpu.VMEM((frames, width), bf16),
            pltpu.SemaphoreType.DMA((10,)),
        ],
        compiler_params=pltpu.CompilerParams(vmem_limit_bytes=56 * 1024 * 1024),
        name="layers",
    )(
        ends,
        extended,
        masks,
        spans,
        spans.T,
        act,
        conv_kernel,
        enc_gain[None],
        *flat[:4],
        *flat[4:],
        hidden,
        cotangent,
    )


def shards(
    phonemes,
    conv_kernel,
    enc_gain,
    enc_in_weight,
    enc_out_weight,
    proj_weight,
    hidden,
    durations,
    utt_counts,
    timesteps,
    ada_weight,
    ff_in_weight,
    ff_out_weight,
    cotangent,
):
    ctx_index = lax.axis_index("ctx")
    ctx_count = lax.axis_size("ctx")
    dp_count = lax.axis_size("dp")
    phone_rows = phonemes[0]
    phone_local = phone_rows.shape[0]
    frame_local = hidden.shape[1]
    utt_ends = jnp.cumsum(utt_counts[0])
    window_rows = phone_local + 2 * HALO
    extended = extended_2(phone_rows, (("ctx", 0),), HALO + 3)
    positions = ctx_index * phone_local - HALO - 3 + jnp.arange(window_rows + 6, dtype=jnp.int32)
    segment = jnp.sum((utt_ends[None, :] <= positions[:, None]).astype(jnp.int32), axis=1)
    centre = segment[3 : 3 + window_rows]
    masks = jnp.stack(
        [segment[k : k + window_rows] == centre for k in range(7)] + [centre < 0], axis=1
    ).astype(jnp.float32)
    phone_dur = durations[0]
    phone_end = jnp.cumsum(phone_dur)
    phone_begin = phone_end - phone_dur
    begin_padded = jnp.pad(phone_begin, HALO, constant_values=-1)
    end_padded = jnp.pad(phone_end, HALO, constant_values=-1)
    begin_window = lax.dynamic_slice_in_dim(begin_padded, ctx_index * phone_local, window_rows)
    end_window = lax.dynamic_slice_in_dim(end_padded, ctx_index * phone_local, window_rows)
    spans = jnp.stack([begin_window, end_window]) - ctx_index * frame_local
    utt_marks = (
        jnp.arange(phone_dur.shape[0], dtype=jnp.int32)[None, :] < utt_ends[:, None]
    ).astype(jnp.int32)
    utt_frame_end = jnp.sum(utt_marks * phone_dur[None, :], axis=1)
    act = jax.nn.silu(time_embed(timesteps[0], ada_weight.shape[0])).astype(jnp.bfloat16)
    transformer_layer_output, frame_gradient_rows, window_sums, enc_halves = layers(
        utt_frame_end - ctx_index * frame_local,
        extended,
        masks,
        spans,
        act,
        conv_kernel,
        enc_gain,
        enc_in_weight,
        enc_out_weight,
        proj_weight,
        ada_weight,
        ff_in_weight,
        ff_out_weight,
        hidden,
        cotangent,
        dp_count * ctx_count // 2,
    )
    norm_factor = 1.0 / math.sqrt(dp_count * ctx_count * frame_local)
    encoder_output_gradient, projection_weight_gradient = reduce_gradients(
        enc_halves, window_sums, proj_weight, phone_local, norm_factor
    )
    return (
        transformer_layer_output,
        frame_gradient_rows,
        encoder_output_gradient[None],
        projection_weight_gradient,
    )


def solution(mesh):
    in_specs = (
        P("dp", "ctx", None),
        P(),
        P(),
        P(),
        P(),
        P(),
        P("dp", "ctx", None),
        P("dp", None),
        P("dp", None),
        P("dp", None),
        P(),
        P(),
        P(),
        P("dp", "ctx", None),
    )
    out_specs = (
        P("dp", "ctx", None),
        P("dp", "ctx", None),
        P("dp", "ctx", None),
        P(("dp", "ctx"), None),
    )
    return jax.shard_map(shards, mesh=mesh, in_specs=in_specs, out_specs=out_specs, check_vma=False)
```

```python
import functools
import math

import jax
import jax.numpy as jnp
from jax import lax
from jax.experimental import pallas as pl
from jax.experimental.pallas import tpu as pltpu
from jax.sharding import PartitionSpec as P

HALO = 8
EDGE = 16
UTT_SLOTS = 8
PIECES = 3
WIDE = 512
MESH = pl.DeviceIdType.MESH


tanh_scale = 0.7978845608028654


def gelu_value(inputs):
    inner = tanh_scale * (inputs + 0.044715 * inputs * inputs * inputs)
    return 0.5 * inputs * (1.0 + jnp.tanh(inner))


def time_embed(timestep_ids, width):
    half_width = width // 2
    frequency = jnp.exp(-math.log(10000.0) * jnp.arange(half_width, dtype=jnp.float32) / half_width)
    angles = timestep_ids.astype(jnp.float32)[:, None] * frequency[None, :]
    return jnp.concatenate([jnp.sin(angles), jnp.cos(angles)], axis=1)


def rms_scale(values):
    return lax.rsqrt(jnp.mean(values * values, axis=-1, keepdims=True) + 1e-06)


def contract_cols(left, right):
    return lax.dot_general(
        left, right, (((1,), (1,)), ((), ())), preferred_element_type=jnp.float32
    )


def gelu_parts(inputs):
    squared = inputs * inputs
    hyper = jnp.tanh(tanh_scale * (inputs + 0.044715 * squared * inputs))
    half = 0.5 * (1.0 + hyper)
    slope = half + 0.5 * inputs * (1.0 - hyper * hyper) * tanh_scale * (
        1.0 + 3.0 * 0.044715 * squared
    )
    return inputs * half, slope


def kernel(
    dp_count,
    ctx_count,
    norm_factor,
    counts_ref,
    phone_ref,
    durations_ref,
    act_ref,
    conv_ref,
    gain_ref,
    enc_in_hbm,
    enc_out_hbm,
    proj_hbm,
    ada_hbm,
    ff_in_hbm,
    ff_out_hbm,
    hidden_hbm,
    cot_hbm,
    out_hbm,
    d_hidden_hbm,
    enc_grad_ref,
    proj_grad_ref,
    enc_in,
    enc_out,
    proj,
    ada,
    ff_in,
    ff_out,
    hidden,
    cot,
    halo_low,
    halo_high,
    ext32,
    segment,
    parts,
    resid,
    normed2,
    d_mlp,
    hidact,
    d_pre,
    out_buf,
    d_hidden,
    halves,
    sums,
    sums16,
    pair_enc,
    pair_sums,
    from_low,
    from_high,
    terms,
    first_in,
    second_out,
    second_in,
    chip_out,
    chip_in,
    load_sem,
    halo_send,
    halo_recv,
    edge_send,
    edge_recv,
    enc_send,
    enc_recv,
    pair_send,
    pair_recv,
    first_send,
    first_recv,
    second_send,
    second_recv,
    chip_send,
    chip_recv,
):
    bf16, f32 = jnp.bfloat16, jnp.float32
    d = lax.axis_index("dp")
    c = lax.axis_index("ctx")
    core = lax.rem(c, 2)
    chip = c // 2
    chips = ctx_count // 2
    pair = c + 1 - 2 * core
    after = lax.rem(c + 1, ctx_count)
    before = lax.rem(c + ctx_count - 1, ctx_count)
    other = lax.rem(c + ctx_count - 1 + 2 * core, ctx_count)
    by_low = d + 1 - 2 * lax.rem(d, 2)
    by_high = lax.rem(d + dp_count // 2, dp_count)
    near = jnp.where(core == 0, by_low, by_high)
    far = jnp.where(core == 0, by_high, by_low)
    opposite = dp_count - 1 - d
    pieces, _, group_rows, cols = terms.shape
    rows = group_rows // chips
    phones = phone_ref.shape[1]
    window = sums.shape[0]
    frames, width = resid.shape
    inner_width = hidact.shape[1]
    utts = counts_ref.shape[1]
    groups = dp_count * chips
    slots = 2 * UTT_SLOTS

    barrier = pltpu.get_barrier_semaphore()
    partners = [(d, pair), (d, other), (near, c), (far, c)]
    for i in range(1, chips):
        partners.append((d, lax.rem(c + 2 * i, ctx_count)))
    for partner in partners:
        pl.semaphore_signal(barrier, inc=1, device_id=partner, device_id_type=MESH)
    loaded = {}
    order = (
        (ada_hbm, ada),
        (cot_hbm.at[0], cot),
        (enc_in_hbm, enc_in),
        (enc_out_hbm, enc_out),
        (proj_hbm, proj),
        (hidden_hbm.at[0], hidden),
        (ff_in_hbm, ff_in),
        (ff_out_hbm, ff_out),
    )
    names = ("ada", "cot", "enc_in", "enc_out", "proj", "hidden", "ff_in", "ff_out")
    for i, (src, dst) in enumerate(order):
        loaded[names[i]] = pltpu.make_async_copy(src, dst, load_sem.at[i])
        loaded[names[i]].start()

    def remote(src, dst, send, recv, target):
        return pltpu.make_async_remote_copy(
            src_ref=src,
            dst_ref=dst,
            send_sem=send,
            recv_sem=recv,
            device_id=target,
            device_id_type=MESH,
        )

    pl.semaphore_wait(barrier, len(partners))
    halo_copies = [
        remote(
            phone_ref.at[0, phones - EDGE :], halo_low, halo_send.at[0], halo_recv.at[0], (d, after)
        ),
        remote(phone_ref.at[0, :EDGE], halo_high, halo_send.at[1], halo_recv.at[1], (d, before)),
    ]
    for copy in halo_copies:
        copy.start()

    ends = [counts_ref[0, 0]]
    for u in range(1, utts):
        ends.append(ends[u - 1] + counts_ref[0, u])
    total_phones = durations_ref.shape[1]
    spread = jnp.broadcast_to(durations_ref[...].astype(f32), (slots, total_phones)).astype(bf16)
    phone = lax.broadcasted_iota(jnp.int32, (window, total_phones), 1)
    place = c * phones - HALO + lax.broadcasted_iota(jnp.int32, (window, total_phones), 0)
    is_before = jnp.where(phone < place, 1.0, 0.0).astype(bf16)
    up_to = jnp.where(phone <= place, 1.0, 0.0).astype(bf16)
    slot = lax.broadcasted_iota(jnp.int32, (slots, total_phones), 0) % UTT_SLOTS
    low = jnp.zeros((slots, total_phones), jnp.int32)
    high = low
    for u in range(utts):
        low = jnp.where(slot == u, ends[u - 1] if u else 0, low)
        high = jnp.where(slot == u, ends[u], high)
    phone = lax.broadcasted_iota(jnp.int32, (slots, total_phones), 1)
    utt_low = contract_cols(spread, jnp.where(phone < low, 1.0, 0.0).astype(bf16))
    utt_high = contract_cols(spread, jnp.where(phone < high, 1.0, 0.0).astype(bf16))
    base = c * frames
    frame = (base + lax.broadcasted_iota(jnp.int32, (frames, slots), 0)).astype(f32)
    utt_onehot = jnp.where((frame >= utt_low[0:1, :]) & (frame < utt_high[0:1, :]), 1.0, 0.0)
    utt_onehot16 = utt_onehot.astype(bf16)
    frame = (base + lax.broadcasted_iota(jnp.int32, (frames, window), 0)).astype(f32)
    onehot = jnp.where(
        (frame >= contract_cols(spread, is_before)[0:1, :])
        & (frame < contract_cols(spread, up_to)[0:1, :]),
        1.0,
        0.0,
    ).astype(bf16)
    frame = (base + lax.broadcasted_iota(jnp.int32, (window, frames), 1)).astype(f32)
    turned_onehot = jnp.where(
        (frame >= contract_cols(is_before, spread)[:, 0:1])
        & (frame < contract_cols(up_to, spread)[:, 0:1]),
        1.0,
        0.0,
    ).astype(bf16)

    loaded["ada"].wait()
    for at in range(0, 3 * width, cols):
        modul = jnp.dot(act_ref[...], ada[:, at : at + cols], preferred_element_type=f32)
        upper = modul.astype(bf16).astype(f32)
        row = lax.broadcasted_iota(jnp.int32, (slots, cols), 0)
        parts[:, at : at + cols] = jnp.where(row < UTT_SLOTS, upper, modul - upper).astype(bf16)

    def pick(which, at):
        start = which * width + at
        return jnp.dot(utt_onehot16, parts[:, start : start + cols], preferred_element_type=f32)

    normed2[frames:, :] = parts[:, :width]
    loaded["cot"].wait()
    for at in range(0, width, cols):
        d_mlp[:, at : at + cols] = (pick(2, at) * cot[:, at : at + cols].astype(f32)).astype(bf16)

    position = c * phones - EDGE + lax.broadcasted_iota(jnp.int32, segment.shape, 0)
    number = jnp.where(position < 0, -1, 0)
    for u in range(utts):
        number = number + jnp.where(position >= ends[u], 1, 0)
    segment[...] = number
    ext32[EDGE : EDGE + phones, :] = phone_ref[0].astype(f32)
    for copy in halo_copies:
        copy.wait_recv()
    ext32[:EDGE, :] = halo_low[...].astype(f32)
    ext32[EDGE + phones :, :] = halo_high[...].astype(f32)
    shift = EDGE - HALO
    masks = [
        jnp.where(
            segment[shift + k - 3 : shift + k - 3 + window, :] == segment[shift : shift + window, :],
            1.0,
            0.0,
        )
        for k in range(7)
    ]
    lanes = segment.shape[1]
    mixed_parts = []
    for at in range(0, ext32.shape[1], lanes):
        mixed = jnp.zeros((window, lanes), f32)
        for k in range(7):
            mixed = (
                mixed
                + conv_ref[k : k + 1, at : at + lanes]
                * ext32[shift + k - 3 : shift + k - 3 + window, at : at + lanes]
                * masks[k]
            )
        mixed_parts.append(mixed)
    mixed = jnp.concatenate(mixed_parts, axis=1)
    normed = (mixed * rms_scale(mixed) * gain_ref[...]).astype(bf16)
    loaded["enc_in"].wait()
    inner = gelu_value(jnp.dot(normed, enc_in[...], preferred_element_type=f32)).astype(bf16)
    loaded["enc_out"].wait()
    encoded = (
        ext32[shift : shift + window, :]
        + jnp.dot(inner, enc_out[...], preferred_element_type=f32)
    ).astype(bf16)
    turned = encoded.astype(f32).T.reshape(groups, 2, rows, window)
    for half in range(2):
        halves[half] = turned[:, half].reshape(groups * rows, window).astype(bf16)
    enc_copy = remote(
        halves.at[1 - core], pair_enc, enc_send.at[0], enc_recv.at[0], (d, pair)
    )
    enc_copy.start()
    loaded["proj"].wait()
    cond = jnp.dot(encoded, proj[...], preferred_element_type=f32).astype(bf16)

    loaded["hidden"].wait()
    square = jnp.zeros((frames, 1), f32)
    for at in range(0, width, cols):
        value = hidden[:, at : at + cols].astype(f32) + jnp.dot(
            onehot, cond[:, at : at + cols], preferred_element_type=f32
        )
        resid[:, at : at + cols] = value
        square = square + jnp.sum(value * value, axis=-1, keepdims=True)
    square = square * (1.0 / width) + 1e-06
    rinv = lax.rsqrt(square)
    for at in range(0, width, cols):
        normed2[:frames, at : at + cols] = (
            resid[:, at : at + cols] * rinv * (1.0 + pick(1, at)) + pick(0, at)
        ).astype(bf16)
    loaded["ff_in"].wait()
    loaded["ff_out"].wait()
    inside = jnp.zeros((frames, 1), f32)
    for at in range(0, inner_width, WIDE):
        here = slice(at, at + WIDE)
        both = jnp.dot(normed2[...], ff_in[:, here], preferred_element_type=f32)
        pre = both[:frames]
        value, slope = gelu_parts(pre)
        hidact[:, here] = value.astype(bf16)
        grad = (contract_cols(d_mlp[...], ff_out[here, :]) * slope).astype(bf16)
        d_pre[:, here] = grad
        of_shift = contract_cols(grad, both[frames:].astype(bf16)) * utt_onehot
        inside = (
            inside
            + jnp.sum(grad.astype(f32) * pre, axis=-1, keepdims=True)
            - jnp.sum(of_shift, axis=-1, keepdims=True)
        )
    factor = rinv * rinv * inside * (1.0 / width)

    first = {}
    pair_copies = []

    def send_terms(q):
        at = slice(q * cols, (q + 1) * cols)
        pair_copies[q].wait_recv()
        if q == 0:
            enc_copy.wait_recv()
        term = jnp.dot(halves[core], sums16[q], preferred_element_type=f32)
        term = term + jnp.dot(pair_enc[...], pair_sums[q], preferred_element_type=f32)
        terms[q] = term.astype(bf16).reshape(dp_count, group_rows, cols)
        for i, group in ((1, opposite), (0, near)):
            first[q, i] = remote(
                terms.at[q, group],
                first_in.at[q, i],
                first_send.at[q, i],
                first_recv.at[q, i],
                (near, c),
            )
            first[q, i].start()

    for q in range(pieces):
        at = slice(q * cols, (q + 1) * cols)
        d_hat = contract_cols(d_pre[...], ff_in[at, :]) * (1.0 + pick(1, q * cols))
        d_hidden[:, at] = (
            cot[:, at].astype(f32) + rinv * d_hat - resid[:, at] * factor
        ).astype(bf16)
        piece = jnp.dot(turned_onehot, d_hidden[:, at], preferred_element_type=f32)
        sums[:, at] = piece
        sums16[q] = piece.astype(bf16)
        pair_copies.append(
            remote(sums16.at[q], pair_sums.at[q], pair_send.at[q], pair_recv.at[q], (d, pair))
        )
        pair_copies[q].start()
        if q >= 1:
            send_terms(q - 1)
    edge_copies = [
        remote(sums.at[:HALO], from_high, edge_send.at[0], edge_recv.at[0], (d, before)),
        remote(sums.at[window - HALO :], from_low, edge_send.at[1], edge_recv.at[1], (d, after)),
    ]
    for copy in edge_copies:
        copy.start()
    d_store = pltpu.make_async_copy(d_hidden, d_hidden_hbm.at[0], load_sem.at[8])
    d_store.start()
    send_terms(pieces - 1)

    second = []
    chip_copies = []
    for q in range(pieces + 1):
        if q < pieces:
            at = slice(q * cols, (q + 1) * cols)
            mlp = jnp.dot(hidact[...], ff_out[:, at], preferred_element_type=f32)
            out_buf[:, at] = (resid[:, at] + pick(2, q * cols) * mlp).astype(bf16)
            first[q, 1].wait_recv()
            second_out[q] = (terms[q, far].astype(f32) + first_in[q, 1].astype(f32)).astype(bf16)
            second.append(
                remote(
                    second_out.at[q],
                    second_in.at[q],
                    second_send.at[q],
                    second_recv.at[q],
                    (far, c),
                )
            )
            second[q].start()
        if q >= 1:
            p = q - 1
            first[p, 0].wait_recv()
            second[p].wait_recv()
            total = (
                terms[p, d].astype(f32) + first_in[p, 0].astype(f32) + second_in[p].astype(f32)
            )
            chip_out[p] = total.reshape(chips, rows, cols).astype(bf16)
            for i in range(1, chips):
                target = lax.rem(chip + i, chips)
                copy = remote(
                    chip_out.at[p, target],
                    chip_in.at[p, i],
                    chip_send.at[p, i],
                    chip_recv.at[p, i],
                    (d, 2 * target + core),
                )
                copy.start()
                chip_copies.append((p, i, copy))
        if q == pieces - 1:
            out_store = pltpu.make_async_copy(out_buf, out_hbm.at[0], load_sem.at[9])
            out_store.start()
            for copy in edge_copies:
                copy.wait_recv()
            own = sums[HALO : HALO + phones, :]
            d_cond = jnp.concatenate(
                [
                    own[:HALO] + from_low[...],
                    own[HALO : phones - HALO],
                    own[phones - HALO :] + from_high[...],
                ],
                axis=0,
            ).astype(bf16)
            enc_grad_ref[...] = contract_cols(d_cond, proj[...]).astype(bf16)
    for q in range(pieces):
        total = chip_out[q, chip].astype(f32)
        for p, i, copy in chip_copies:
            if p == q:
                copy.wait_recv()
                total = total + chip_in[q, i].astype(f32)
        proj_grad_ref[:, q * cols : (q + 1) * cols] = total * norm_factor
    for copy in halo_copies + [enc_copy] + edge_copies + pair_copies + second:
        copy.wait_send()
    for copy in first.values():
        copy.wait_send()
    for _, _, copy in chip_copies:
        copy.wait_send()
    out_store.wait()
    d_store.wait()


def shards(
    phonemes,
    conv_kernel,
    enc_gain,
    enc_in_weight,
    enc_out_weight,
    proj_weight,
    hidden,
    durations,
    utt_counts,
    timesteps,
    ada_weight,
    ff_in_weight,
    ff_out_weight,
    cotangent,
):
    dp_count, ctx_count = lax.axis_size("dp"), lax.axis_size("ctx")
    chips = ctx_count // 2
    phones, enc_width = phonemes.shape[1:]
    frames, width = hidden.shape[1:]
    inner_width = ff_in_weight.shape[1]
    window = phones + 2 * HALO
    rows = enc_width // (dp_count * ctx_count)
    group_rows = chips * rows
    cols = width // PIECES
    slots = 2 * UTT_SLOTS
    steps = jnp.pad(timesteps[0], (0, UTT_SLOTS - timesteps.shape[1]))
    act = jax.nn.silu(time_embed(jnp.concatenate([steps, steps]), ada_weight.shape[0])).astype(
        jnp.bfloat16
    )
    norm_factor = 1.0 / math.sqrt(dp_count * ctx_count * frames)
    vmem = pl.BlockSpec(memory_space=pltpu.VMEM)
    hbm = pl.BlockSpec(memory_space=pl.ANY)
    bf16, f32, dma = jnp.bfloat16, jnp.float32, pltpu.SemaphoreType.DMA
    weights = (enc_in_weight, enc_out_weight, proj_weight, ada_weight, ff_in_weight, ff_out_weight)
    out, d_hidden, enc_grad, proj_grad = pl.pallas_call(
        functools.partial(kernel, dp_count, ctx_count, norm_factor),
        out_shape=(
            jax.ShapeDtypeStruct(hidden.shape, bf16),
            jax.ShapeDtypeStruct(hidden.shape, bf16),
            jax.ShapeDtypeStruct((phones, enc_width), bf16),
            jax.ShapeDtypeStruct((rows, width), f32),
        ),
        in_specs=[pl.BlockSpec(memory_space=pltpu.SMEM)] + [vmem] * 5 + [hbm] * 8,
        out_specs=(hbm, hbm, vmem, vmem),
        scratch_shapes=[pltpu.VMEM(a.shape, bf16) for a in weights]
        + [
            pltpu.VMEM((frames, width), bf16),
            pltpu.VMEM((frames, width), bf16),
            pltpu.VMEM((EDGE, enc_width), bf16),
            pltpu.VMEM((EDGE, enc_width), bf16),
            pltpu.VMEM((phones + 2 * EDGE, enc_width), f32),
            pltpu.VMEM((phones + 2 * EDGE, 128), jnp.int32),
            pltpu.VMEM((slots, 3 * width), bf16),
            pltpu.VMEM((frames, width), f32),
            pltpu.VMEM((frames + slots, width), bf16),
            pltpu.VMEM((frames, width), bf16),
            pltpu.VMEM((frames, inner_width), bf16),
            pltpu.VMEM((frames, inner_width), bf16),
            pltpu.VMEM((frames, width), bf16),
            pltpu.VMEM((frames, width), bf16),
            pltpu.VMEM((2, enc_width // 2, window), bf16),
            pltpu.VMEM((window, width), f32),
            pltpu.VMEM((PIECES, window, cols), bf16),
            pltpu.VMEM((enc_width // 2, window), bf16),
            pltpu.VMEM((PIECES, window, cols), bf16),
            pltpu.VMEM((HALO, width), f32),
            pltpu.VMEM((HALO, width), f32),
            pltpu.VMEM((PIECES, dp_count, group_rows, cols), bf16),
            pltpu.VMEM((PIECES, 2, group_rows, cols), bf16),
            pltpu.VMEM((PIECES, group_rows, cols), bf16),
            pltpu.VMEM((PIECES, group_rows, cols), bf16),
            pltpu.VMEM((PIECES, chips, rows, cols), bf16),
            pltpu.VMEM((PIECES, chips, rows, cols), bf16),
            dma((10,)),
            dma((2,)),
            dma((2,)),
            dma((2,)),
            dma((2,)),
            dma((1,)),
            dma((1,)),
            dma((PIECES,)),
            dma((PIECES,)),
            dma((PIECES, 2)),
            dma((PIECES, 2)),
            dma((PIECES,)),
            dma((PIECES,)),
            dma((PIECES, chips)),
            dma((PIECES, chips)),
        ],
        compiler_params=pltpu.CompilerParams(
            collective_id=0, has_side_effects=True, vmem_limit_bytes=60 * 1024 * 1024
        ),
        name="layers",
    )(
        utt_counts,
        phonemes,
        durations,
        act,
        conv_kernel,
        enc_gain[None],
        *weights,
        hidden,
        cotangent,
    )
    return out, d_hidden, enc_grad[None], proj_grad


def solution(mesh):
    in_specs = (
        P("dp", "ctx", None),
        P(),
        P(),
        P(),
        P(),
        P(),
        P("dp", "ctx", None),
        P("dp", None),
        P("dp", None),
        P("dp", None),
        P(),
        P(),
        P(),
        P("dp", "ctx", None),
    )
    out_specs = (
        P("dp", "ctx", None),
        P("dp", "ctx", None),
        P("dp", "ctx", None),
        P(("dp", "ctx"), None),
    )
    return jax.shard_map(shards, mesh=mesh, in_specs=in_specs, out_specs=out_specs, check_vma=False)
```

```python
import functools
import math

import jax
import jax.numpy as jnp
from jax import lax
from jax.experimental import pallas as pl
from jax.experimental.pallas import tpu as pltpu
from jax.sharding import PartitionSpec as P

HALO = 8
EDGE = 16
UTT_SLOTS = 8
PIECES = 6
WIDE = 512
MESH = pl.DeviceIdType.MESH


tanh_scale = 0.7978845608028654


def gelu_value(inputs):
    inner = tanh_scale * (inputs + 0.044715 * inputs * inputs * inputs)
    return 0.5 * inputs * (1.0 + jnp.tanh(inner))


def time_embed(timestep_ids, width):
    half_width = width // 2
    frequency = jnp.exp(-math.log(10000.0) * jnp.arange(half_width, dtype=jnp.float32) / half_width)
    angles = timestep_ids.astype(jnp.float32)[:, None] * frequency[None, :]
    return jnp.concatenate([jnp.sin(angles), jnp.cos(angles)], axis=1)


def rms_scale(values):
    return lax.rsqrt(jnp.mean(values * values, axis=-1, keepdims=True) + 1e-06)


def contract_cols(left, right):
    return lax.dot_general(
        left, right, (((1,), (1,)), ((), ())), preferred_element_type=jnp.float32
    )


def gelu_parts(inputs):
    squared = inputs * inputs
    hyper = jnp.tanh(tanh_scale * (inputs + 0.044715 * squared * inputs))
    half = 0.5 * (1.0 + hyper)
    slope = half + 0.5 * inputs * (1.0 - hyper * hyper) * tanh_scale * (
        1.0 + 3.0 * 0.044715 * squared
    )
    return inputs * half, slope


def kernel(
    dp_count,
    ctx_count,
    norm_factor,
    counts_ref,
    phone_ref,
    durations_ref,
    act_ref,
    conv_ref,
    gain_ref,
    enc_in_hbm,
    enc_out_hbm,
    proj_hbm,
    ada_hbm,
    ff_in_hbm,
    ff_out_hbm,
    hidden_hbm,
    cot_hbm,
    out_ref,
    d_hidden_ref,
    enc_grad_ref,
    proj_grad_ref,
    enc_in,
    enc_out,
    proj,
    ada,
    ff_in,
    ff_out,
    hidden,
    cot,
    halo_low,
    halo_high,
    ext32,
    segment,
    parts,
    resid,
    normed2,
    d_mlp,
    hidact,
    d_pre,
    halves,
    sums,
    sums16,
    pair_enc,
    pair_sums,
    from_low,
    from_high,
    terms,
    first_in,
    second_out,
    second_in,
    chip_out,
    chip_in,
    load_sem,
    halo_send,
    halo_recv,
    edge_send,
    edge_recv,
    enc_send,
    enc_recv,
    pair_send,
    pair_recv,
    first_send,
    first_recv,
    second_send,
    second_recv,
    chip_send,
    chip_recv,
):
    bf16, f32 = jnp.bfloat16, jnp.float32
    d = lax.axis_index("dp")
    c = lax.axis_index("ctx")
    core = lax.rem(c, 2)
    chip = c // 2
    chips = ctx_count // 2
    pair = c + 1 - 2 * core
    after = lax.rem(c + 1, ctx_count)
    before = lax.rem(c + ctx_count - 1, ctx_count)
    other = lax.rem(c + ctx_count - 1 + 2 * core, ctx_count)
    by_low = d + 1 - 2 * lax.rem(d, 2)
    by_high = lax.rem(d + dp_count // 2, dp_count)
    near = jnp.where(core == 0, by_low, by_high)
    far = jnp.where(core == 0, by_high, by_low)
    opposite = dp_count - 1 - d
    pieces, _, group_rows, cols = terms.shape
    rows = group_rows // chips
    phones = phone_ref.shape[1]
    window = sums.shape[0]
    frames, width = resid.shape
    inner_width = hidact.shape[1]
    utts = counts_ref.shape[1]
    groups = dp_count * chips
    slots = 2 * UTT_SLOTS

    barrier = pltpu.get_barrier_semaphore()
    partners = [(d, pair), (d, other), (near, c), (far, c)]
    for i in range(1, chips):
        partners.append((d, lax.rem(c + 2 * i, ctx_count)))
    for partner in partners:
        pl.semaphore_signal(barrier, inc=1, device_id=partner, device_id_type=MESH)
    loaded = {}
    order = (
        (ada_hbm, ada),
        (cot_hbm.at[0], cot),
        (enc_in_hbm, enc_in),
        (enc_out_hbm, enc_out),
        (proj_hbm, proj),
        (hidden_hbm.at[0], hidden),
        (ff_in_hbm, ff_in),
        (ff_out_hbm, ff_out),
    )
    names = ("ada", "cot", "enc_in", "enc_out", "proj", "hidden", "ff_in", "ff_out")
    for i, (src, dst) in enumerate(order):
        loaded[names[i]] = pltpu.make_async_copy(src, dst, load_sem.at[i])
        loaded[names[i]].start()

    def remote(src, dst, send, recv, target):
        return pltpu.make_async_remote_copy(
            src_ref=src,
            dst_ref=dst,
            send_sem=send,
            recv_sem=recv,
            device_id=target,
            device_id_type=MESH,
        )

    ends = [counts_ref[0, 0]]
    for u in range(1, utts):
        ends.append(ends[u - 1] + counts_ref[0, u])
    total_phones = durations_ref.shape[1]
    spread = jnp.broadcast_to(durations_ref[...].astype(f32), (slots, total_phones)).astype(bf16)
    phone = lax.broadcasted_iota(jnp.int32, (window, total_phones), 1)
    place = c * phones - HALO + lax.broadcasted_iota(jnp.int32, (window, total_phones), 0)
    is_before = jnp.where(phone < place, 1.0, 0.0).astype(bf16)
    up_to = jnp.where(phone <= place, 1.0, 0.0).astype(bf16)
    slot = lax.broadcasted_iota(jnp.int32, (slots, total_phones), 0) % UTT_SLOTS
    low = jnp.zeros((slots, total_phones), jnp.int32)
    high = low
    for u in range(utts):
        low = jnp.where(slot == u, ends[u - 1] if u else 0, low)
        high = jnp.where(slot == u, ends[u], high)
    phone = lax.broadcasted_iota(jnp.int32, (slots, total_phones), 1)
    utt_low = contract_cols(spread, jnp.where(phone < low, 1.0, 0.0).astype(bf16))
    utt_high = contract_cols(spread, jnp.where(phone < high, 1.0, 0.0).astype(bf16))
    base = c * frames
    frame = (base + lax.broadcasted_iota(jnp.int32, (frames, slots), 0)).astype(f32)
    utt_onehot = jnp.where((frame >= utt_low[0:1, :]) & (frame < utt_high[0:1, :]), 1.0, 0.0)
    utt_onehot16 = utt_onehot.astype(bf16)
    frame = (base + lax.broadcasted_iota(jnp.int32, (frames, window), 0)).astype(f32)
    onehot = jnp.where(
        (frame >= contract_cols(spread, is_before)[0:1, :])
        & (frame < contract_cols(spread, up_to)[0:1, :]),
        1.0,
        0.0,
    ).astype(bf16)
    frame = (base + lax.broadcasted_iota(jnp.int32, (window, frames), 1)).astype(f32)
    turned_onehot = jnp.where(
        (frame >= contract_cols(is_before, spread)[:, 0:1])
        & (frame < contract_cols(up_to, spread)[:, 0:1]),
        1.0,
        0.0,
    ).astype(bf16)

    pl.semaphore_wait(barrier, len(partners))
    halo_copies = [
        remote(
            phone_ref.at[0, phones - EDGE :], halo_low, halo_send.at[0], halo_recv.at[0], (d, after)
        ),
        remote(phone_ref.at[0, :EDGE], halo_high, halo_send.at[1], halo_recv.at[1], (d, before)),
    ]
    for copy in halo_copies:
        copy.start()

    loaded["ada"].wait()
    blank = jnp.zeros((UTT_SLOTS - utts, act_ref.shape[1]), f32)
    act = act_ref[...].astype(f32)
    act = jnp.concatenate([act, blank, act, blank], axis=0).astype(bf16)
    for at in range(0, 3 * width, cols):
        modul = jnp.dot(act, ada[:, at : at + cols], preferred_element_type=f32)
        upper = modul.astype(bf16).astype(f32)
        row = lax.broadcasted_iota(jnp.int32, (slots, cols), 0)
        parts[:, at : at + cols] = jnp.where(row < UTT_SLOTS, upper, modul - upper).astype(bf16)

    def pick(which, at):
        start = which * width + at
        return jnp.dot(utt_onehot16, parts[:, start : start + cols], preferred_element_type=f32)

    normed2[frames:, :] = parts[:, :width]
    loaded["cot"].wait()
    for at in range(0, width, cols):
        d_mlp[:, at : at + cols] = (pick(2, at) * cot[:, at : at + cols].astype(f32)).astype(bf16)

    position = c * phones - EDGE + lax.broadcasted_iota(jnp.int32, segment.shape, 0)
    number = jnp.where(position < 0, -1, 0)
    for u in range(utts):
        number = number + jnp.where(position >= ends[u], 1, 0)
    segment[...] = number
    ext32[EDGE : EDGE + phones, :] = phone_ref[0].astype(f32)
    for copy in halo_copies:
        copy.wait_recv()
    ext32[:EDGE, :] = halo_low[...].astype(f32)
    ext32[EDGE + phones :, :] = halo_high[...].astype(f32)
    shift = EDGE - HALO
    masks = [
        jnp.where(
            segment[shift + k - 3 : shift + k - 3 + window, :] == segment[shift : shift + window, :],
            1.0,
            0.0,
        )
        for k in range(7)
    ]
    lanes = segment.shape[1]
    mixed_parts = []
    for at in range(0, ext32.shape[1], lanes):
        mixed = jnp.zeros((window, lanes), f32)
        for k in range(7):
            mixed = (
                mixed
                + conv_ref[k : k + 1, at : at + lanes]
                * ext32[shift + k - 3 : shift + k - 3 + window, at : at + lanes]
                * masks[k]
            )
        mixed_parts.append(mixed)
    mixed = jnp.concatenate(mixed_parts, axis=1)
    normed = (mixed * rms_scale(mixed) * gain_ref[...]).astype(bf16)
    loaded["enc_in"].wait()
    inner = gelu_value(jnp.dot(normed, enc_in[...], preferred_element_type=f32)).astype(bf16)
    loaded["enc_out"].wait()
    encoded = (
        ext32[shift : shift + window, :]
        + jnp.dot(inner, enc_out[...], preferred_element_type=f32)
    ).astype(bf16)
    turned = encoded.astype(f32).T.reshape(groups, 2, rows, window)
    for half in range(2):
        halves[half] = turned[:, half].reshape(groups * rows, window).astype(bf16)
    enc_copy = remote(
        halves.at[1 - core], pair_enc, enc_send.at[0], enc_recv.at[0], (d, pair)
    )
    enc_copy.start()
    loaded["proj"].wait()
    cond = jnp.dot(encoded, proj[...], preferred_element_type=f32).astype(bf16)

    loaded["hidden"].wait()
    square = jnp.zeros((frames, 1), f32)
    for at in range(0, width, cols):
        value = hidden[:, at : at + cols].astype(f32) + jnp.dot(
            onehot, cond[:, at : at + cols], preferred_element_type=f32
        )
        resid[:, at : at + cols] = value
        square = square + jnp.sum(value * value, axis=-1, keepdims=True)
    square = square * (1.0 / width) + 1e-06
    rinv = lax.rsqrt(square)
    for at in range(0, width, cols):
        normed2[:frames, at : at + cols] = (
            resid[:, at : at + cols] * rinv * (1.0 + pick(1, at)) + pick(0, at)
        ).astype(bf16)
    loaded["ff_in"].wait()
    loaded["ff_out"].wait()
    inside = jnp.zeros((frames, 1), f32)
    for at in range(0, inner_width, WIDE):
        here = slice(at, at + WIDE)
        both = jnp.dot(normed2[...], ff_in[:, here], preferred_element_type=f32)
        pre = both[:frames]
        value, slope = gelu_parts(pre)
        hidact[:, here] = value.astype(bf16)
        grad = (contract_cols(d_mlp[...], ff_out[here, :]) * slope).astype(bf16)
        d_pre[:, here] = grad
        of_shift = contract_cols(grad, both[frames:].astype(bf16)) * utt_onehot
        inside = (
            inside
            + jnp.sum(grad.astype(f32) * pre, axis=-1, keepdims=True)
            - jnp.sum(of_shift, axis=-1, keepdims=True)
        )
    factor = rinv * rinv * inside * (1.0 / width)

    first = {}
    pair_copies = []

    def send_terms(q):
        at = slice(q * cols, (q + 1) * cols)
        pair_copies[q].wait_recv()
        if q == 0:
            enc_copy.wait_recv()
        term = jnp.dot(halves[core], sums16[q], preferred_element_type=f32)
        term = term + jnp.dot(pair_enc[...], pair_sums[q], preferred_element_type=f32)
        terms[q] = term.astype(bf16).reshape(dp_count, group_rows, cols)
        for i, group in ((1, opposite), (0, near)):
            first[q, i] = remote(
                terms.at[q, group],
                first_in.at[q, i],
                first_send.at[q, i],
                first_recv.at[q, i],
                (near, c),
            )
            first[q, i].start()

    for q in range(pieces):
        at = slice(q * cols, (q + 1) * cols)
        d_hat = contract_cols(d_pre[...], ff_in[at, :]) * (1.0 + pick(1, q * cols))
        d_hidden_ref[0, :, at] = (
            cot[:, at].astype(f32) + rinv * d_hat - resid[:, at] * factor
        ).astype(bf16)
        piece = jnp.dot(turned_onehot, d_hidden_ref[0, :, at], preferred_element_type=f32)
        sums[:, at] = piece
        sums16[q] = piece.astype(bf16)
        pair_copies.append(
            remote(sums16.at[q], pair_sums.at[q], pair_send.at[q], pair_recv.at[q], (d, pair))
        )
        pair_copies[q].start()
        if q >= 1:
            send_terms(q - 1)
    edge_copies = [
        remote(sums.at[:HALO], from_high, edge_send.at[0], edge_recv.at[0], (d, before)),
        remote(sums.at[window - HALO :], from_low, edge_send.at[1], edge_recv.at[1], (d, after)),
    ]
    for copy in edge_copies:
        copy.start()
    send_terms(pieces - 1)

    second = []
    chip_copies = []
    for q in range(pieces + 1):
        if q < pieces:
            at = slice(q * cols, (q + 1) * cols)
            mlp = jnp.dot(hidact[...], ff_out[:, at], preferred_element_type=f32)
            out_ref[0, :, at] = (resid[:, at] + pick(2, q * cols) * mlp).astype(bf16)
            first[q, 1].wait_recv()
            second_out[q] = (terms[q, far].astype(f32) + first_in[q, 1].astype(f32)).astype(bf16)
            second.append(
                remote(
                    second_out.at[q],
                    second_in.at[q],
                    second_send.at[q],
                    second_recv.at[q],
                    (far, c),
                )
            )
            second[q].start()
        if q >= 1:
            p = q - 1
            first[p, 0].wait_recv()
            second[p].wait_recv()
            total = (
                terms[p, d].astype(f32) + first_in[p, 0].astype(f32) + second_in[p].astype(f32)
            )
            chip_out[p] = total.reshape(chips, rows, cols).astype(bf16)
            for i in range(1, chips):
                target = lax.rem(chip + i, chips)
                copy = remote(
                    chip_out.at[p, target],
                    chip_in.at[p, i],
                    chip_send.at[p, i],
                    chip_recv.at[p, i],
                    (d, 2 * target + core),
                )
                copy.start()
                chip_copies.append((p, i, copy))
        if q == pieces - 1:
            for copy in edge_copies:
                copy.wait_recv()
            own = sums[HALO : HALO + phones, :]
            d_cond = jnp.concatenate(
                [
                    own[:HALO] + from_low[...],
                    own[HALO : phones - HALO],
                    own[phones - HALO :] + from_high[...],
                ],
                axis=0,
            ).astype(bf16)
            enc_grad_ref[...] = contract_cols(d_cond, proj[...]).astype(bf16)
    for q in range(pieces):
        total = chip_out[q, chip].astype(f32)
        for p, i, copy in chip_copies:
            if p == q:
                copy.wait_recv()
                total = total + chip_in[q, i].astype(f32)
        proj_grad_ref[:, q * cols : (q + 1) * cols] = total * norm_factor
    for copy in halo_copies + [enc_copy] + edge_copies + pair_copies + second:
        copy.wait_send()
    for copy in first.values():
        copy.wait_send()
    for _, _, copy in chip_copies:
        copy.wait_send()


def shards(
    phonemes,
    conv_kernel,
    enc_gain,
    enc_in_weight,
    enc_out_weight,
    proj_weight,
    hidden,
    durations,
    utt_counts,
    timesteps,
    ada_weight,
    ff_in_weight,
    ff_out_weight,
    cotangent,
):
    dp_count, ctx_count = lax.axis_size("dp"), lax.axis_size("ctx")
    chips = ctx_count // 2
    phones, enc_width = phonemes.shape[1:]
    frames, width = hidden.shape[1:]
    inner_width = ff_in_weight.shape[1]
    window = phones + 2 * HALO
    rows = enc_width // (dp_count * ctx_count)
    group_rows = chips * rows
    cols = width // PIECES
    slots = 2 * UTT_SLOTS
    act = jax.nn.silu(time_embed(timesteps[0], ada_weight.shape[0])).astype(jnp.bfloat16)
    norm_factor = 1.0 / math.sqrt(dp_count * ctx_count * frames)
    vmem = pl.BlockSpec(memory_space=pltpu.VMEM)
    hbm = pl.BlockSpec(memory_space=pl.ANY)
    bf16, f32, dma = jnp.bfloat16, jnp.float32, pltpu.SemaphoreType.DMA
    weights = (enc_in_weight, enc_out_weight, proj_weight, ada_weight, ff_in_weight, ff_out_weight)
    out, d_hidden, enc_grad, proj_grad = pl.pallas_call(
        functools.partial(kernel, dp_count, ctx_count, norm_factor),
        out_shape=(
            jax.ShapeDtypeStruct(hidden.shape, bf16),
            jax.ShapeDtypeStruct(hidden.shape, bf16),
            jax.ShapeDtypeStruct((phones, enc_width), bf16),
            jax.ShapeDtypeStruct((rows, width), f32),
        ),
        in_specs=[pl.BlockSpec(memory_space=pltpu.SMEM)] + [vmem] * 5 + [hbm] * 8,
        out_specs=(vmem,) * 4,
        scratch_shapes=[pltpu.VMEM(a.shape, bf16) for a in weights]
        + [
            pltpu.VMEM((frames, width), bf16),
            pltpu.VMEM((frames, width), bf16),
            pltpu.VMEM((EDGE, enc_width), bf16),
            pltpu.VMEM((EDGE, enc_width), bf16),
            pltpu.VMEM((phones + 2 * EDGE, enc_width), f32),
            pltpu.VMEM((phones + 2 * EDGE, 128), jnp.int32),
            pltpu.VMEM((slots, 3 * width), bf16),
            pltpu.VMEM((frames, width), f32),
            pltpu.VMEM((frames + slots, width), bf16),
            pltpu.VMEM((frames, width), bf16),
            pltpu.VMEM((frames, inner_width), bf16),
            pltpu.VMEM((frames, inner_width), bf16),
            pltpu.VMEM((2, enc_width // 2, window), bf16),
            pltpu.VMEM((window, width), f32),
            pltpu.VMEM((PIECES, window, cols), bf16),
            pltpu.VMEM((enc_width // 2, window), bf16),
            pltpu.VMEM((PIECES, window, cols), bf16),
            pltpu.VMEM((HALO, width), f32),
            pltpu.VMEM((HALO, width), f32),
            pltpu.VMEM((PIECES, dp_count, group_rows, cols), bf16),
            pltpu.VMEM((PIECES, 2, group_rows, cols), bf16),
            pltpu.VMEM((PIECES, group_rows, cols), bf16),
            pltpu.VMEM((PIECES, group_rows, cols), bf16),
            pltpu.VMEM((PIECES, chips, rows, cols), bf16),
            pltpu.VMEM((PIECES, chips, rows, cols), bf16),
            dma((8,)),
            dma((2,)),
            dma((2,)),
            dma((2,)),
            dma((2,)),
            dma((1,)),
            dma((1,)),
            dma((PIECES,)),
            dma((PIECES,)),
            dma((PIECES, 2)),
            dma((PIECES, 2)),
            dma((PIECES,)),
            dma((PIECES,)),
            dma((PIECES, chips)),
            dma((PIECES, chips)),
        ],
        compiler_params=pltpu.CompilerParams(
            collective_id=0, has_side_effects=True, vmem_limit_bytes=49 * 1024 * 1024
        ),
        name="layers",
    )(
        utt_counts,
        phonemes,
        durations,
        act,
        conv_kernel,
        enc_gain[None],
        *weights,
        hidden,
        cotangent,
    )
    return out, d_hidden, enc_grad[None], proj_grad


def solution(mesh):
    in_specs = (
        P("dp", "ctx", None),
        P(),
        P(),
        P(),
        P(),
        P(),
        P("dp", "ctx", None),
        P("dp", None),
        P("dp", None),
        P("dp", None),
        P(),
        P(),
        P(),
        P("dp", "ctx", None),
    )
    out_specs = (
        P("dp", "ctx", None),
        P("dp", "ctx", None),
        P("dp", "ctx", None),
        P(("dp", "ctx"), None),
    )
    return jax.shard_map(shards, mesh=mesh, in_specs=in_specs, out_specs=out_specs, check_vma=False)
```
